256 devices in a mesh: dp: 16 (over y, z_hi), fsdp: 16 (over x, z_lo, core).
Axes of the slice: x: 4, y: 4, z: 8 (z_hi: 4, z_lo: 2; z = z_hi * 2 + z_lo), core: 2. Of those that a mesh axis runs over, the one named last changes fastest.
Arguments:
- layer_input: bfloat16 [24576, 4096], P('dp', 'fsdp'), may hold values from -6 to 6
- grad_out: bfloat16 [24576, 14336], P('dp', 'fsdp'), may hold values from -0.0546875 to 0.0546875
- subspace: bfloat16 [4096, 1024], P('fsdp'), may hold values from -0.09375 to 0.09375
- up_weight: bfloat16 [16, 896, 4096], P('fsdp', 'dp'), may hold values from -0.09375 to 0.09375
- first_moment: float32 [16, 896, 1024], P('fsdp', 'dp'), may hold values from -4 to 4
- second_moment: float32 [16, 896, 1024], P('fsdp', 'dp'), may hold values from 0.01 to 1
Outputs:
- new_weight: bfloat16 [16, 896, 4096], P(None, 'dp')
- new_first: float32 [16, 896, 1024], P('fsdp', 'dp')
- new_second: float32 [16, 896, 1024], P('fsdp', 'dp')
The draws below stay inside these ranges and needn't reach their ends.
All inputs are finite; a program needn't handle non-finite values.
Results may differ from the reference program's by a relative error of at most 0.0025.
Values may be sent and summed in bfloat16 or wider, within the bound.
A program may use at most 64 MiB of HBM per device.

```python
import math
import jax
import jax.numpy as jnp
from jax import lax

D = 4096
FF = 14336
R = 1024
TOKENS = 24576
BLOCK = 896
N_FSDP = 16


def strengthened(drawn, own_key, source, target, shards_of, factor):
    def block_of(position):
        return (jnp.arange(drawn.shape[position]) // (drawn.shape[position] // shards_of)).reshape((-1,) + (1,) * (drawn.ndim - 1 - position))

    near = jax.random.permutation(own_key, shards_of)[block_of(target)]
    second = (block_of(target) + shards_of // 2) % shards_of
    return jnp.where((block_of(source) == near) | (block_of(source) == second), factor * drawn, drawn)


def block_scale(own_key, extent, shards, low, largest):
    gain, own = 1.0, jax.random.fold_in(own_key, 6)
    for axis_at, blocks in shards:
        heights = jnp.exp(jax.random.uniform(jax.random.fold_in(own, axis_at), (blocks,), jnp.float32, low / len(shards), largest / len(shards)))
        gain = gain * jnp.repeat(heights, extent[axis_at] // blocks).reshape([-1 if axis == axis_at else 1 for axis in range(len(extent))])
    return gain


def bell_draw(stream_key, extent, spread, reach, shards=(), dtype=jnp.bfloat16):
    values = jax.random.normal(stream_key, extent, jnp.float32) * spread
    if len(shards) > 0:
        values = block_scale(stream_key, extent, shards, -0.22, 0.18) * values
    return jnp.clip(values, min=-reach, max=reach).astype(dtype)


def noise_with(stream_key, extent, spread, most, pieces, heavy, kind=jnp.bfloat16):
    array = spread * jax.random.normal(stream_key, extent, jnp.float32)
    if pieces:
        array = array * block_scale(stream_key, extent, pieces, -0.22, 0.18)
    return jnp.clip(strengthened(array, jax.random.fold_in(stream_key, 3), *heavy), -most, most).astype(kind)


def setup_inputs(seed: int = 0) -> dict:
    splits = jax.random.split(jax.random.key(seed), 7)
    layer_input = bell_draw(splits[0], (TOKENS, D), 1.0, 6.0, ((0, 16), (1, 16)))
    grad_out = noise_with(splits[1], (TOKENS, FF), TOKENS ** -0.5, 0.0546875, ((0, 16), (1, 16)), (0, 1, 16, 2.0))
    subspace = bell_draw(splits[2], (D, R), D ** -0.5, 0.09375, ((0, 16),))
    up_weight = bell_draw(splits[3], (N_FSDP, BLOCK, D), D ** -0.5, 0.09375, ((0, 16), (1, 16)))
    first_moment = bell_draw(splits[4], (N_FSDP, BLOCK, R), 0.3, 4.0, ((0, 16), (1, 16)), jnp.float32)
    second_moment = jnp.clip(jnp.exp(math.log(1.0) - 4.6051702 * jax.random.uniform(splits[5], (N_FSDP, BLOCK, R), jnp.float32) ** block_scale(splits[5], (N_FSDP, BLOCK, R), ((0, 16), (1, 16)), -0.2, 0.2)), 0.01, 1.0)
    return dict(layer_input=layer_input, grad_out=grad_out, subspace=subspace, up_weight=up_weight, first_moment=first_moment, second_moment=second_moment)


beta_one = 0.9
beta_two = 0.999
bias_one = 1.0 - 0.9 ** 10
bias_two = 1.0 - 0.999 ** 10
epsilon = 1e-08
step_size = 0.05

def reference(layer_input, grad_out, subspace, up_weight, first_moment, second_moment):
    coords = jnp.dot(layer_input, subspace, preferred_element_type=jnp.float32).astype(jnp.bfloat16)
    projected = lax.dot_general(grad_out, coords, (((0,), (0,)), ((), ())), preferred_element_type=jnp.float32)
    projected = projected.reshape(N_FSDP, BLOCK, R)
    new_first = beta_one * first_moment + (1.0 - beta_one) * projected
    new_second = beta_two * second_moment + (1.0 - beta_two) * projected * projected
    direction = (new_first / bias_one / (jnp.sqrt(new_second / bias_two) + epsilon)).astype(jnp.bfloat16)
    change = lax.dot_general(direction.reshape(FF, R), subspace, (((1,), (1,)), ((), ())), preferred_element_type=jnp.float32)
    change = change.reshape(N_FSDP, BLOCK, D)
    new_weight = (up_weight.astype(jnp.float32) - step_size * change).astype(jnp.bfloat16)
    return (new_weight, new_first, new_second)
```

```python
import jax
import jax.numpy as jnp
from jax import lax
from jax.experimental import pallas as pl
from jax.experimental.pallas import tpu as pltpu
from jax.sharding import PartitionSpec as P

beta_one = 0.9
beta_two = 0.999
bias_one = 1.0 - 0.9**10
bias_two = 1.0 - 0.999**10
epsilon = 1e-08
step_size = 0.05

MESH = pl.DeviceIdType.MESH
BF = jnp.bfloat16
F32 = jnp.float32

TOK = 1536
OWN = 96
DIN = 256
R = 1024
HID = 896
UNITS = 56
YROWS = 224
HALF = 512


def body(
    x_hbm, g_hbm, s_hbm, w_hbm, m_ref, v_ref,
    s_out, w_out, d_out, p_out,
    s_all, x_all, g_v, gt, c_all, acc, ysend, yrecv, yown, zrecv, d_own,
    loc, s_ss, s_rs, x_ss, x_rs, c_ss, c_rs, w_ss, w_rs, d_ss, d_rs, y_ss, y_rs, z_ss, z_rs,
):
    dp = lax.axis_index("dp")
    f = lax.axis_index("fsdp")
    y, zh = dp // 4, dp % 4
    x, zl, c = f // 4, (f // 2) % 2, f % 2

    def slot(dx=0, dz=0, dc=0):
        xx = (x + dx) % 4
        zz = (zl + dz) % 2
        cc = (c + dc) % 2
        return xx * 4 + zz * 2 + cc

    def fdev(dx=0, dz=0, dc=0):
        return (dp, slot(dx, dz, dc))

    def ydev(dy):
        return (((y + dy) % 4) * 4 + zh, f)

    def zdev(dz):
        return (y * 4 + (zh + dz) % 4, f)

    pair = fdev(dz=1)
    other = (y * 4 + (zh + 3 + 2 * zl) % 4, slot(dz=1))
    mate = fdev(dc=1)

    load_g = pltpu.make_async_copy(g_hbm, g_v, loc.at[0])
    load_g.start()
    load_s = pltpu.make_async_copy(s_hbm, s_all.at[f], loc.at[1])
    load_s.start()
    load_x = pltpu.make_async_copy(x_hbm.at[pl.ds(f * OWN, OWN)], x_all.at[f], loc.at[2])
    load_x.start()
    load_w = pltpu.make_async_copy(w_hbm, w_out.at[f], loc.at[3])
    load_w.start()

    bar = pltpu.get_barrier_semaphore()

    def greet(k, _):
        pl.semaphore_signal(bar, inc=1, device_id=(dp, (f + k) % 16), device_id_type=MESH)
        return 0

    lax.fori_loop(1, 16, greet, 0)
    for k in (1, 2, 3):
        pl.semaphore_signal(bar, inc=1, device_id=ydev(k), device_id_type=MESH)
        pl.semaphore_signal(bar, inc=1, device_id=zdev(k), device_id_type=MESH)
    pl.semaphore_signal(bar, inc=1, device_id=other, device_id_type=MESH)
    pl.semaphore_wait(bar, 22)

    def send(src, dst, ss, rs, i, to):
        cp = pltpu.make_async_remote_copy(
            src_ref=src, dst_ref=dst, send_sem=ss.at[i], recv_sem=rs.at[i],
            device_id=to, device_id_type=MESH,
        )
        cp.start()
        return cp

    def arrived(dst, ss, rs, i):
        pltpu.make_async_remote_copy(
            src_ref=dst, dst_ref=dst, send_sem=ss.at[i], recv_sem=rs.at[i],
            device_id=mate, device_id_type=MESH,
        ).wait_recv()

    yp = y % 2
    mine = pl.ds(pl.multiple_of(yp * 128, 128), 128)
    mine0 = pl.ds(pl.multiple_of(yp * 128, 64), 64)
    mine1 = pl.ds(pl.multiple_of(yp * 128 + 64, 64), 64)
    his = pl.ds(pl.multiple_of((1 - yp) * 128, 128), 128)
    his0 = pl.ds(pl.multiple_of((1 - yp) * 128, 64), 64)
    his1 = pl.ds(pl.multiple_of((1 - yp) * 128 + 64, 64), 64)
    sent = []

    def s_send(src, dst, i, to):
        sent.append(send(src, dst, s_ss, s_rs, i, to))

    s_send(s_hbm.at[mine0], s_all.at[f, mine0], 0, pair)
    s_send(s_hbm.at[mine1], s_all.at[f, mine1], 1, other)
    for dx in (1, 3, 2):
        s_send(s_hbm.at[mine], s_all.at[f, mine], 1 + dx, fdev(dx=dx))
    s_send(s_hbm, s_all.at[f], 5, mate)

    zs = slot(dz=1)
    arrived(s_all.at[zs, mine0], s_ss, s_rs, 0)
    arrived(s_all.at[zs, mine1], s_ss, s_rs, 1)
    for dx in (1, 3, 2):
        s_send(s_all.at[zs, mine], s_all.at[zs, mine], 5 + dx, fdev(dx=dx))

    def s_forward(q, base):
        s_send(s_all.at[q, mine0], s_all.at[q, mine0], base, ydev(1))
        s_send(s_all.at[q, mine1], s_all.at[q, mine1], base + 1, ydev(3))
        s_send(s_all.at[q, mine], s_all.at[q, mine], base + 2, mate)

    s_forward(zs, 9)

    def x_send(k, _):
        p = (f + k) % 16
        send(x_hbm.at[pl.ds(p * OWN, OWN)], x_all.at[f], x_ss, x_rs, k, (dp, p))
        return 0

    lax.fori_loop(1, 16, x_send, 0)

    load_g.wait()

    def turn(t, _):
        at = pl.ds(pl.multiple_of(t * 128, 128), 128)
        gt[:, at] = g_v[at, :].T
        return 0

    for n, dx in enumerate((1, 3, 2)):
        q = slot(dx=4 - dx)
        arrived(s_all.at[q, mine], s_ss, s_rs, 1 + dx)
        s_forward(q, 12 + 3 * n)
        lax.fori_loop(2 * n, 2 * n + 2, turn, 0)
    for n, dx in enumerate((1, 3, 2)):
        q = slot(dx=4 - dx, dz=1)
        arrived(s_all.at[q, mine], s_ss, s_rs, 5 + dx)
        s_forward(q, 21 + 3 * n)
        lax.fori_loop(6 + 2 * n, 8 + 2 * n, turn, 0)
    forwarded = [(0, 1, 9)]
    forwarded += [(4 - dx, 0, 12 + 3 * n) for n, dx in enumerate((1, 3, 2))]
    forwarded += [(4 - dx, 1, 21 + 3 * n) for n, dx in enumerate((1, 3, 2))]
    for n, (dx, dz, base) in enumerate(forwarded):
        q = slot(dx=dx, dz=dz)
        arrived(s_all.at[q, his0], s_ss, s_rs, base)
        arrived(s_all.at[q, his1], s_ss, s_rs, base + 1)
        s_send(s_all.at[q, his], s_all.at[q, his], 30 + n, mate)
    arrived(s_all.at[slot(dc=1)], s_ss, s_rs, 5)
    for n, (dx, dz, base) in enumerate(forwarded):
        q = slot(dx=dx, dz=dz, dc=1)
        arrived(s_all.at[q, mine], s_ss, s_rs, base + 2)
        arrived(s_all.at[q, his], s_ss, s_rs, 30 + n)

    def x_wait(k, _):
        arrived(x_all.at[(f + 16 - k) % 16], x_ss, x_rs, k)
        return 0

    lax.fori_loop(1, 16, x_wait, 0)
    load_s.wait()
    load_x.wait()
    keep_s = pltpu.make_async_copy(s_all, s_out, loc.at[4])
    keep_s.start()

    acc[...] = jnp.zeros_like(acc)

    def add(i, _):
        acc[...] += jnp.dot(x_all[i], s_all[i], preferred_element_type=F32)
        return 0

    lax.fori_loop(0, 16, add, 0)

    def rows(q):
        return pl.ds(pl.multiple_of(q * OWN, 32), OWN)

    c_all[rows(f), :] = acc[...].astype(BF)

    def gather(own, at, ss, rs):
        done = []

        def go(src, dst, i, to):
            done.append(send(src, dst, ss, rs, i, to))

        def start():
            go(own, at(f), 0, pair)
            for dx in (1, 3, 2):
                go(own, at(f), dx, fdev(dx=dx))
            go(own, at(f), 4, mate)

        def turn_z():
            arrived(at(zs), ss, rs, 0)
            for dx in (1, 3, 2):
                go(at(zs), at(zs), 4 + dx, fdev(dx=dx))
            go(at(zs), at(zs), 8, mate)

        def pass_on():
            for dz, base in ((0, 0), (1, 4)):
                for dx in (1, 3, 2):
                    q = slot(dx=4 - dx, dz=dz)
                    arrived(at(q), ss, rs, base + dx)
                    go(at(q), at(q), 8 + dx + 3 * dz, mate)

        def finish():
            arrived(at(slot(dc=1)), ss, rs, 4)
            arrived(at(slot(dz=1, dc=1)), ss, rs, 8)
            for dz in (0, 1):
                for dx in (1, 3, 2):
                    arrived(at(slot(dx=4 - dx, dz=dz, dc=1)), ss, rs, 8 + dx + 3 * dz)

        def drain():
            for cp in done:
                cp.wait_send()

        return start, turn_z, pass_on, finish, drain

    c_start, c_turn, c_pass, c_finish, c_drain = gather(
        c_all.at[rows(f)], lambda q: c_all.at[rows(q)], c_ss, c_rs
    )
    w_start, w_turn, w_pass, w_finish, w_drain = gather(
        w_hbm, lambda q: w_out.at[q], w_ss, w_rs
    )
    d_start, d_turn, d_pass, d_finish, d_drain = gather(
        d_own, lambda q: d_out.at[q], d_ss, d_rs
    )
    c_start()
    c_turn()
    w_start()
    c_pass()
    c_finish()

    def block(k, h):
        t = (y + k) % 4
        a = gt[pl.ds(pl.multiple_of(t * YROWS, 32), YROWS), :]
        return jnp.dot(a, c_all[:, h * HALF:(h + 1) * HALF], preferred_element_type=F32)

    ysent = []
    for h in range(2):
        for k in (1, 3, 2):
            ysend[h, k - 1] = block(k, h).astype(BF)
            ysent.append(send(ysend.at[h, k - 1], yrecv.at[h, k - 1], y_ss, y_rs, 3 * h + k - 1, ydev(k)))
        yown[h] = block(0, h)
    w_turn()

    zsent = []
    for h in range(2):
        for k in (1, 3, 2):
            arrived(yrecv.at[h, k - 1], y_ss, y_rs, 3 * h + k - 1)
        yown[h] = yown[h] + yrecv[h, 0].astype(F32) + yrecv[h, 1].astype(F32) + yrecv[h, 2].astype(F32)
        for k in (1, 3, 2):
            t = (zh + k) % 4
            src = yown.at[h, pl.ds(pl.multiple_of(t * UNITS, 8), UNITS)]
            zsent.append(send(src, zrecv.at[h, k - 1], z_ss, z_rs, 3 * h + k - 1, zdev(k)))
    for h in range(2):
        cols = slice(h * HALF, (h + 1) * HALF)
        for k in (1, 3, 2):
            arrived(zrecv.at[h, k - 1], z_ss, z_rs, 3 * h + k - 1)
        got = yown[h, pl.ds(pl.multiple_of(zh * UNITS, 8), UNITS), :]
        got = got + zrecv[h, 0] + zrecv[h, 1] + zrecv[h, 2]
        p_out[:, cols] = got
        one = beta_one * m_ref[:, cols] + (1.0 - beta_one) * got
        two = beta_two * v_ref[:, cols] + (1.0 - beta_two) * got * got
        d_own[:, cols] = (one / bias_one / (jnp.sqrt(two / bias_two) + epsilon)).astype(BF)
    keep_d = pltpu.make_async_copy(d_own, d_out.at[f], loc.at[5])
    keep_d.start()
    d_start()
    d_turn()
    w_pass()
    d_pass()
    w_finish()
    d_finish()

    for cp in sent + ysent + zsent:
        cp.wait_send()

    def x_sent(k, _):
        pltpu.make_async_remote_copy(
            src_ref=x_hbm.at[pl.ds(0, OWN)], dst_ref=x_all.at[0], send_sem=x_ss.at[k], recv_sem=x_rs.at[k],
            device_id=mate, device_id_type=MESH,
        ).wait_send()
        return 0

    lax.fori_loop(1, 16, x_sent, 0)
    c_drain()
    w_drain()
    d_drain()
    load_w.wait()
    keep_s.wait()
    keep_d.wait()


def exchange(layer_input, grad_out, subspace, up_weight, first, second):
    hbm = pl.BlockSpec(memory_space=pl.ANY)
    vmem = pl.BlockSpec(memory_space=pltpu.VMEM)
    dma = pltpu.SemaphoreType.DMA
    return pl.pallas_call(
        body,
        out_shape=(
            jax.ShapeDtypeStruct((16, DIN, R), BF),
            jax.ShapeDtypeStruct((16, UNITS, 4096), BF),
            jax.ShapeDtypeStruct((16, UNITS, R), BF),
            jax.ShapeDtypeStruct((UNITS, R), F32),
        ),
        in_specs=[hbm, hbm, hbm, hbm, vmem, vmem],
        out_specs=(hbm, hbm, hbm, vmem),
        scratch_shapes=[
            pltpu.VMEM((16, DIN, R), BF),
            pltpu.VMEM((16, OWN, DIN), BF),
            pltpu.VMEM((TOK, HID), BF),
            pltpu.VMEM((HID, TOK), BF),
            pltpu.VMEM((TOK, R), BF),
            pltpu.VMEM((OWN, R), F32),
            pltpu.VMEM((2, 3, YROWS, HALF), BF),
            pltpu.VMEM((2, 3, YROWS, HALF), BF),
            pltpu.VMEM((2, YROWS, HALF), F32),
            pltpu.VMEM((2, 3, UNITS, HALF), F32),
            pltpu.VMEM((UNITS, R), BF),
            dma((6,)),
            dma((37,)), dma((37,)),
            dma((16,)), dma((16,)),
            dma((15,)), dma((15,)),
            dma((15,)), dma((15,)),
            dma((15,)), dma((15,)),
            dma((6,)), dma((6,)),
            dma((6,)), dma((6,)),
        ],
        compiler_params=pltpu.CompilerParams(
            collective_id=0, has_side_effects=True, vmem_limit_bytes=40 * 2**20
        ),
        cost_estimate=pl.CostEstimate(flops=4 * 10**9, bytes_accessed=4 * 10**7, transcendentals=0),
        name="exchange",
    )(layer_input, grad_out, subspace, up_weight, first, second)


def local(layer_input, grad_out, subspace, up_weight, first_moment, second_moment):
    basis, weights, direction, projected = exchange(
        layer_input, grad_out, subspace, up_weight[0], first_moment[0], second_moment[0]
    )
    moment_one = beta_one * first_moment[0] + (1.0 - beta_one) * projected
    moment_two = beta_two * second_moment[0] + (1.0 - beta_two) * projected * projected
    change = lax.dot_general(
        direction.reshape(HID, R),
        basis.reshape(4096, R),
        (((1,), (1,)), ((), ())),
        preferred_element_type=F32,
    )
    updated = (weights.reshape(HID, 4096).astype(F32) - step_size * change).astype(BF)
    return (updated.reshape(16, UNITS, 4096), moment_one[None], moment_two[None])


def solution(mesh):
    placed = (
        P("dp", "fsdp"),
        P("dp", "fsdp"),
        P("fsdp", None),
        P("fsdp", "dp", None),
        P("fsdp", "dp", None),
        P("fsdp", "dp", None),
    )
    return jax.shard_map(
        local,
        mesh=mesh,
        in_specs=placed,
        out_specs=(P(None, "dp", None), P("fsdp", "dp", None), P("fsdp", "dp", None)),
        check_vma=False,
    )
```

```python
import jax
import jax.numpy as jnp
from jax import lax
from jax.experimental import pallas as pl
from jax.experimental.pallas import tpu as pltpu
from jax.sharding import PartitionSpec as P

beta_one = 0.9
beta_two = 0.999
bias_one = 1.0 - 0.9**10
bias_two = 1.0 - 0.999**10
epsilon = 1e-08
step_size = 0.05

MESH = pl.DeviceIdType.MESH
BF = jnp.bfloat16
F32 = jnp.float32

TOK = 1536
OWN = 96
DIN = 256
R = 1024
HID = 896
UNITS = 56
YROWS = 224
HALF = 512
PARTS = 4
PART = R // PARTS


def body(
    x_hbm, g_hbm, s_hbm, w_hbm, m_hbm, v_hbm,
    s_out, w_out, d_out, p_out,
    s_all, x_all, g_v, gt, c_all, acc, ysend, yrecv, yown, zrecv, d_own, m_ref, v_ref, w_own,
    loc, s_ss, s_rs, x_ss, x_rs, c_ss, c_rs, w_ss, w_rs, d_ss, d_rs, y_ss, y_rs, z_ss, z_rs,
):
    dp = lax.axis_index("dp")
    f = lax.axis_index("fsdp")
    y, zh = dp // 4, dp % 4
    x, zl, c = f // 4, (f // 2) % 2, f % 2

    def slot(dx=0, dz=0, dc=0):
        xx = (x + dx) % 4
        zz = (zl + dz) % 2
        cc = (c + dc) % 2
        return xx * 4 + zz * 2 + cc

    def fdev(dx=0, dz=0, dc=0):
        return (dp, slot(dx, dz, dc))

    def ydev(dy):
        return (((y + dy) % 4) * 4 + zh, f)

    def zdev(dz):
        return (y * 4 + (zh + dz) % 4, f)

    pair = fdev(dz=1)
    other = (y * 4 + (zh + 3 + 2 * zl) % 4, slot(dz=1))
    mate = fdev(dc=1)

    load_g = pltpu.make_async_copy(g_hbm, g_v, loc.at[0])
    load_g.start()
    load_s = pltpu.make_async_copy(s_hbm, s_all.at[f], loc.at[1])
    load_s.start()
    load_x = pltpu.make_async_copy(x_hbm.at[pl.ds(f * OWN, OWN)], x_all.at[f], loc.at[2])
    load_x.start()
    load_w = pltpu.make_async_copy(w_hbm, w_own, loc.at[3])
    load_w.start()

    load_m = pltpu.make_async_copy(m_hbm, m_ref, loc.at[6])
    load_m.start()
    load_v = pltpu.make_async_copy(v_hbm, v_ref, loc.at[7])
    load_v.start()

    bar = pltpu.get_barrier_semaphore()

    def greet(k, _):
        pl.semaphore_signal(bar, inc=1, device_id=(dp, (f + k) % 16), device_id_type=MESH)
        return 0

    lax.fori_loop(1, 16, greet, 0)
    for k in (1, 2, 3):
        pl.semaphore_signal(bar, inc=1, device_id=ydev(k), device_id_type=MESH)
        pl.semaphore_signal(bar, inc=1, device_id=zdev(k), device_id_type=MESH)
    pl.semaphore_signal(bar, inc=1, device_id=other, device_id_type=MESH)
    pl.semaphore_wait(bar, 22)

    def send(src, dst, ss, rs, i, to):
        cp = pltpu.make_async_remote_copy(
            src_ref=src, dst_ref=dst, send_sem=ss.at[i], recv_sem=rs.at[i],
            device_id=to, device_id_type=MESH,
        )
        cp.start()
        return cp

    def arrived(dst, ss, rs, i):
        pltpu.make_async_remote_copy(
            src_ref=dst, dst_ref=dst, send_sem=ss.at[i], recv_sem=rs.at[i],
            device_id=mate, device_id_type=MESH,
        ).wait_recv()

    sent, ysent, zsent = [], [], []
    even = (y + zl) % 2

    def half(e, n=0, size=128):
        return pl.ds(pl.multiple_of(e * 128 + n, 32), size)

    mine, his = half(even), half(1 - even)

    def s_send(src, at, i, to):
        sent.append(send(src, at, s_ss, s_rs, i, to))

    zs = slot(dz=1)
    s_send(s_hbm.at[half(1 - even, 0, 64)], s_all.at[f, half(1 - even, 0, 64)], 0, pair)
    s_send(s_hbm.at[half(1 - even, 64, 64)], s_all.at[f, half(1 - even, 64, 64)], 1, other)
    s_send(s_hbm.at[mine], s_all.at[f, mine], 2, fdev(dx=1))
    s_send(s_hbm.at[mine], s_all.at[f, mine], 3, fdev(dx=3))
    s_send(s_hbm.at[half(even, 64, 32)], s_all.at[f, half(even, 64, 32)], 4, pair)
    s_send(s_hbm.at[half(even, 96, 32)], s_all.at[f, half(even, 96, 32)], 5, other)
    s_send(s_hbm, s_all.at[f], 6, mate)

    arrived(s_all.at[zs, half(even, 0, 64)], s_ss, s_rs, 0)
    arrived(s_all.at[zs, half(even, 64, 64)], s_ss, s_rs, 1)
    s_send(s_all.at[zs, mine], s_all.at[zs, mine], 7, fdev(dx=1))
    s_send(s_all.at[zs, mine], s_all.at[zs, mine], 8, fdev(dx=3))
    s_send(s_all.at[zs, half(even, 0, 32)], s_all.at[zs, half(even, 0, 32)], 9, ydev(1))
    s_send(s_all.at[zs, half(even, 32, 32)], s_all.at[zs, half(even, 32, 32)], 10, ydev(3))
    s_send(s_all.at[zs, mine], s_all.at[zs, mine], 11, mate)

    around = (ydev(1), ydev(3), pair, other)

    def s_around(q, base):
        for n, to in enumerate(around):
            part = half(even, 32 * n, 32)
            s_send(s_all.at[q, part], s_all.at[q, part], base + n, to)
        s_send(s_all.at[q, mine], s_all.at[q, mine], base + 4, mate)

    load_g.wait()

    def turn(t, _):
        at = pl.ds(pl.multiple_of(t * 128, 128), 128)
        gt[:, at] = g_v[at, :].T
        return 0

    by_x = []
    for dz in (0, 1):
        a, b = slot(dx=3, dz=dz), slot(dx=1, dz=dz)
        arrived(s_all.at[a, mine], s_ss, s_rs, 2 + 5 * dz)
        part = half(even, 0, 64)
        s_send(s_all.at[a, part], s_all.at[a, part], 12 + 2 * dz, fdev(dx=1))
        arrived(s_all.at[b, mine], s_ss, s_rs, 3 + 5 * dz)
        part = half(even, 64, 64)
        s_send(s_all.at[b, part], s_all.at[b, part], 13 + 2 * dz, fdev(dx=3))
        s_around(a, 20 + 14 * dz)
        s_around(b, 27 + 14 * dz)
        by_x += [(3, dz, 20 + 14 * dz), (1, dz, 27 + 14 * dz)]
        lax.fori_loop(4 * dz, 4 * dz + 4, turn, 0)

    def x_send(k, _):
        p = (f + k) % 16
        send(x_hbm.at[pl.ds(p * OWN, OWN)], x_all.at[f], x_ss, x_rs, k, (dp, p))
        return 0

    lax.fori_loop(1, 16, x_send, 0)

    for dz in (0, 1):
        q = slot(dx=2, dz=dz)
        arrived(s_all.at[q, half(even, 0, 64)], s_ss, s_rs, 12 + 2 * dz)
        arrived(s_all.at[q, half(even, 64, 64)], s_ss, s_rs, 13 + 2 * dz)
        s_around(q, 48 + 7 * dz)
        by_x += [(2, dz, 48 + 7 * dz)]
    lax.fori_loop(8, 12, turn, 0)

    q = zs
    arrived(s_all.at[q, half(1 - even, 64, 32)], s_ss, s_rs, 4)
    arrived(s_all.at[q, half(1 - even, 96, 32)], s_ss, s_rs, 5)
    arrived(s_all.at[q, half(1 - even, 0, 32)], s_ss, s_rs, 9)
    arrived(s_all.at[q, half(1 - even, 32, 32)], s_ss, s_rs, 10)
    s_send(s_all.at[q, his], s_all.at[q, his], 16, mate)
    base_of = {(dx, dz): base for dx, dz, base in by_x}
    for dx, dz, base in by_x:
        q = slot(dx=dx, dz=dz)
        for n in range(4):
            came = base_of[dx, dz if n < 2 else 1 - dz] + n
            arrived(s_all.at[q, half(1 - even, 32 * n, 32)], s_ss, s_rs, came)
        s_send(s_all.at[q, his], s_all.at[q, his], base + 5, mate)
    arrived(s_all.at[slot(dc=1)], s_ss, s_rs, 6)
    arrived(s_all.at[slot(dz=1, dc=1), mine], s_ss, s_rs, 11)
    arrived(s_all.at[slot(dz=1, dc=1), his], s_ss, s_rs, 16)
    for dx, dz, base in by_x:
        q = slot(dx=dx, dz=dz, dc=1)
        arrived(s_all.at[q, mine], s_ss, s_rs, base + 4)
        arrived(s_all.at[q, his], s_ss, s_rs, base + 5)

    def x_wait(k, _):
        arrived(x_all.at[(f + 16 - k) % 16], x_ss, x_rs, k)
        return 0

    lax.fori_loop(1, 16, x_wait, 0)
    def x_sent(k, _):
        pltpu.make_async_remote_copy(
            src_ref=x_hbm.at[pl.ds(0, OWN)], dst_ref=x_all.at[0], send_sem=x_ss.at[k], recv_sem=x_rs.at[k],
            device_id=mate, device_id_type=MESH,
        ).wait_send()
        return 0

    lax.fori_loop(1, 16, x_sent, 0)
    load_s.wait()
    load_x.wait()
    load_m.wait()
    load_v.wait()
    keep_s = pltpu.make_async_copy(s_all, s_out, loc.at[4])
    keep_s.start()

    acc[...] = jnp.zeros_like(acc)

    def add(i, _):
        acc[...] += jnp.dot(x_all[i], s_all[i], preferred_element_type=F32)
        return 0

    lax.fori_loop(0, 16, add, 0)

    def rows(q):
        return pl.ds(pl.multiple_of(q * OWN, 32), OWN)

    c_all[rows(f), :] = acc[...].astype(BF)

    def gather(own, at, ss, rs):
        done = []

        def go(src, dst, i, to):
            done.append(send(src, dst, ss, rs, i, to))

        def start():
            go(own, at(f), 0, pair)
            go(own, at(f), 1, fdev(dx=1))
            go(own, at(f), 2, fdev(dx=3))
            go(own, at(f), 3, mate)

        def turn_z():
            arrived(at(zs), ss, rs, 0)
            go(at(zs), at(zs), 4, fdev(dx=1))
            go(at(zs), at(zs), 5, fdev(dx=3))
            go(at(zs), at(zs), 6, mate)

        def pass_on(dz):
            base = 7 + 5 * dz
            a, b = slot(dx=3, dz=dz), slot(dx=1, dz=dz)
            arrived(at(a), ss, rs, 1 + 3 * dz)
            go(at(a, 0), at(a, 0), base, fdev(dx=1))
            arrived(at(b), ss, rs, 2 + 3 * dz)
            go(at(b, 1), at(b, 1), base + 1, fdev(dx=3))
            go(at(a), at(a), base + 2, mate)
            go(at(b), at(b), base + 3, mate)

        def pass_last(dz):
            base = 7 + 5 * dz
            q = slot(dx=2, dz=dz)
            arrived(at(q, 0), ss, rs, base)
            arrived(at(q, 1), ss, rs, base + 1)
            go(at(q), at(q), base + 4, mate)

        def finish():
            arrived(at(slot(dc=1)), ss, rs, 3)
            arrived(at(slot(dz=1, dc=1)), ss, rs, 6)
            for dz in (0, 1):
                base = 7 + 5 * dz
                arrived(at(slot(dx=3, dz=dz, dc=1)), ss, rs, base + 2)
                arrived(at(slot(dx=1, dz=dz, dc=1)), ss, rs, base + 3)
                arrived(at(slot(dx=2, dz=dz, dc=1)), ss, rs, base + 4)

        def drain():
            for cp in done:
                cp.wait_send()

        return start, turn_z, pass_on, pass_last, finish, drain

    def w_at(q, part=None):
        if part is None:
            return w_out.at[q]
        return w_out.at[q, :, part * 2048:(part + 1) * 2048]

    def span(h, part):
        if part is None:
            return slice(h * HALF, (h + 1) * HALF)
        return slice(h * HALF + part * HALF // 2, h * HALF + (part + 1) * HALF // 2)

    def c_at(h):
        return lambda q, part=None: c_all.at[rows(q), span(h, part)]

    def d_at(h):
        return lambda q, part=None: d_out.at[q, :, span(h, part)]

    cg = [gather(c_at(h)(f), c_at(h), c_ss.at[h], c_rs.at[h]) for h in range(2)]
    dg = [gather(d_own.at[:, span(h, None)], d_at(h), d_ss.at[h], d_rs.at[h]) for h in range(2)]
    w_start, w_turn, w_pass, w_last, w_finish, w_drain = gather(w_hbm, w_at, w_ss, w_rs)
    START, TURN, PASS, LAST, FINISH, DRAIN = range(6)
    def block(k, p):
        t = (y + k) % 4
        a = gt[pl.ds(pl.multiple_of(t * YROWS, 32), YROWS), :]
        return jnp.dot(a, c_all[:, p * PART:(p + 1) * PART], preferred_element_type=F32)

    def y_start(p):
        for k in (1, 3, 2):
            ysend[p, k - 1] = block(k, p).astype(BF)
            ysent.append(send(ysend.at[p, k - 1], yrecv.at[p, k - 1], y_ss, y_rs, 3 * p + k - 1, ydev(k)))
        yown[p] = block(0, p)

    def z_start(p):
        for k in (1, 3, 2):
            arrived(yrecv.at[p, k - 1], y_ss, y_rs, 3 * p + k - 1)
        yown[p] = yown[p] + yrecv[p, 0].astype(F32) + yrecv[p, 1].astype(F32) + yrecv[p, 2].astype(F32)
        for k in (1, 3, 2):
            t = (zh + k) % 4
            src = yown.at[p, pl.ds(pl.multiple_of(t * UNITS, 8), UNITS)]
            zsent.append(send(src, zrecv.at[p, k - 1], z_ss, z_rs, 3 * p + k - 1, zdev(k)))

    def step(p):
        cols = slice(p * PART, (p + 1) * PART)
        for k in (1, 3, 2):
            arrived(zrecv.at[p, k - 1], z_ss, z_rs, 3 * p + k - 1)
        got = yown[p, pl.ds(pl.multiple_of(zh * UNITS, 8), UNITS), :]
        got = got + zrecv[p, 0] + zrecv[p, 1] + zrecv[p, 2]
        p_out[:, cols] = got
        one = beta_one * m_ref[:, cols] + (1.0 - beta_one) * got
        two = beta_two * v_ref[:, cols] + (1.0 - beta_two) * got * got
        d_own[:, cols] = (one / bias_one / (jnp.sqrt(two / bias_two) + epsilon)).astype(BF)

    c0, c1 = cg
    d0, d1 = dg
    c0[START]()
    c0[TURN]()
    c1[START]()
    c1[TURN]()
    c0[PASS](0)
    c0[PASS](1)
    c0[LAST](0)
    c0[LAST](1)
    c1[PASS](0)
    c1[PASS](1)
    w_start()
    load_w.wait()
    keep_w = pltpu.make_async_copy(w_own, w_out.at[f], loc.at[8])
    keep_w.start()
    c0[FINISH]()
    y_start(0)
    y_start(1)
    c1[LAST](0)
    c1[LAST](1)
    c1[FINISH]()
    y_start(2)
    y_start(3)
    w_turn()
    z_start(0)
    z_start(1)
    w_pass(0)
    z_start(2)
    step(0)
    step(1)
    d0[START]()
    z_start(3)
    d0[TURN]()
    w_pass(1)
    step(2)
    step(3)
    d1[START]()
    d0[PASS](0)
    d0[PASS](1)
    d1[TURN]()
    keep_d = pltpu.make_async_copy(d_own, d_out.at[f], loc.at[5])
    keep_d.start()
    w_last(0)
    d0[LAST](0)
    d0[LAST](1)
    d1[PASS](0)
    d1[PASS](1)
    w_last(1)
    d1[LAST](0)
    d1[LAST](1)
    w_finish()
    d0[FINISH]()
    d1[FINISH]()
    keep_d.wait()
    keep_w.wait()
    w_drain()
    for g in cg + dg:
        g[DRAIN]()
    keep_s.wait()
    for cp in sent + ysent + zsent:
        cp.wait_send()


def exchange(layer_input, grad_out, subspace, up_weight, first, second):
    hbm = pl.BlockSpec(memory_space=pl.ANY)
    vmem = pl.BlockSpec(memory_space=pltpu.VMEM)
    dma = pltpu.SemaphoreType.DMA
    return pl.pallas_call(
        body,
        out_shape=(
            jax.ShapeDtypeStruct((16, DIN, R), BF),
            jax.ShapeDtypeStruct((16, UNITS, 4096), BF),
            jax.ShapeDtypeStruct((16, UNITS, R), BF),
            jax.ShapeDtypeStruct((UNITS, R), F32),
        ),
        in_specs=[hbm] * 6,
        out_specs=(hbm, hbm, hbm, vmem),
        scratch_shapes=[
            pltpu.VMEM((16, DIN, R), BF),
            pltpu.VMEM((16, OWN, DIN), BF),
            pltpu.VMEM((TOK, HID), BF),
            pltpu.VMEM((HID, TOK), BF),
            pltpu.VMEM((TOK, R), BF),
            pltpu.VMEM((OWN, R), F32),
            pltpu.VMEM((PARTS, 3, YROWS, PART), BF),
            pltpu.VMEM((PARTS, 3, YROWS, PART), BF),
            pltpu.VMEM((PARTS, YROWS, PART), F32),
            pltpu.VMEM((PARTS, 3, UNITS, PART), F32),
            pltpu.VMEM((UNITS, R), BF),
            pltpu.VMEM((UNITS, R), F32),
            pltpu.VMEM((UNITS, R), F32),
            pltpu.VMEM((UNITS, 4096), BF),
            dma((9,)),
            dma((62,)), dma((62,)),
            dma((16,)), dma((16,)),
            dma((2, 17)), dma((2, 17)),
            dma((17,)), dma((17,)),
            dma((2, 17)), dma((2, 17)),
            dma((3 * PARTS,)), dma((3 * PARTS,)),
            dma((3 * PARTS,)), dma((3 * PARTS,)),
        ],
        compiler_params=pltpu.CompilerParams(
            collective_id=0, has_side_effects=True, vmem_limit_bytes=60 * 2**20
        ),
        cost_estimate=pl.CostEstimate(flops=4 * 10**9, bytes_accessed=4 * 10**7, transcendentals=0),
        name="exchange",
    )(layer_input, grad_out, subspace, up_weight, first, second)


def finish(d_ref, s_ref, w_ref, p_ref, m_ref, v_ref, o_ref, one_ref, two_ref):
    @pl.when(pl.program_id(0) == 0)
    def _():
        got = p_ref[...]
        one_ref[...] = beta_one * m_ref[...] + (1.0 - beta_one) * got
        two_ref[...] = beta_two * v_ref[...] + (1.0 - beta_two) * got * got

    change = lax.dot_general(
        d_ref[...], s_ref[...], (((1,), (1,)), ((), ())), preferred_element_type=F32
    )
    o_ref[...] = (w_ref[...].astype(F32) - step_size * change).astype(BF)


TILE = 1024


def update(direction, basis, weights, projected, first, second):
    whole = pl.BlockSpec((UNITS, R), lambda i: (0, 0))
    return pl.pallas_call(
        finish,
        grid=(4096 // TILE,),
        out_shape=(
            jax.ShapeDtypeStruct((HID, 4096), BF),
            jax.ShapeDtypeStruct((UNITS, R), F32),
            jax.ShapeDtypeStruct((UNITS, R), F32),
        ),
        in_specs=[
            pl.BlockSpec((HID, R), lambda i: (0, 0)),
            pl.BlockSpec((TILE, R), lambda i: (i, 0)),
            pl.BlockSpec((HID, TILE), lambda i: (0, i)),
            whole, whole, whole,
        ],
        out_specs=(pl.BlockSpec((HID, TILE), lambda i: (0, i)), whole, whole),
        compiler_params=pltpu.CompilerParams(vmem_limit_bytes=60 * 2**20),
        cost_estimate=pl.CostEstimate(flops=8 * 10**9, bytes_accessed=26 * 10**6, transcendentals=0),
        name="update",
    )(direction, basis, weights, projected, first, second)


def local(layer_input, grad_out, subspace, up_weight, first_moment, second_moment):
    basis, weights, direction, projected = exchange(
        layer_input, grad_out, subspace, up_weight[0], first_moment[0], second_moment[0]
    )
    updated, moment_one, moment_two = update(
        direction.reshape(HID, R), basis.reshape(4096, R), weights.reshape(HID, 4096),
        projected, first_moment[0], second_moment[0],
    )
    return (updated.reshape(16, UNITS, 4096), moment_one[None], moment_two[None])


def solution(mesh):
    placed = (
        P("dp", "fsdp"),
        P("dp", "fsdp"),
        P("fsdp", None),
        P("fsdp", "dp", None),
        P("fsdp", "dp", None),
        P("fsdp", "dp", None),
    )
    return jax.shard_map(
        local,
        mesh=mesh,
        in_specs=placed,
        out_specs=(P(None, "dp", None), P("fsdp", "dp", None), P("fsdp", "dp", None)),
        check_vma=False,
    )
```

```python
import jax
import jax.numpy as jnp
from jax import lax
from jax.experimental import pallas as pl
from jax.experimental.pallas import tpu as pltpu
from jax.sharding import PartitionSpec as P

beta_one = 0.9
beta_two = 0.999
bias_one = 1.0 - 0.9**10
bias_two = 1.0 - 0.999**10
epsilon = 1e-08
step_size = 0.05

MESH = pl.DeviceIdType.MESH
BF = jnp.bfloat16
F32 = jnp.float32

TOK = 1536
OWN = 96
DIN = 256
R = 1024
HID = 896
UNITS = 56
YROWS = 224
HALF = 512
PARTS = 4
PART = R // PARTS


def body(
    x_hbm, g_hbm, s_hbm, w_hbm, m_hbm, v_hbm,
    s_out, w_out, d_out, p_out,
    s_all, x_all, g_v, gt, c_all, acc, ysend, yrecv, yown, zrecv, d_own, m_ref, v_ref, w_own,
    loc, s_ss, s_rs, x_ss, x_rs, c_ss, c_rs, w_ss, w_rs, d_ss, d_rs, y_ss, y_rs, z_ss, z_rs,
):
    dp = lax.axis_index("dp")
    f = lax.axis_index("fsdp")
    y, zh = dp // 4, dp % 4
    x, zl, c = f // 4, (f // 2) % 2, f % 2

    def slot(dx=0, dz=0, dc=0):
        xx = (x + dx) % 4
        zz = (zl + dz) % 2
        cc = (c + dc) % 2
        return xx * 4 + zz * 2 + cc

    def fdev(dx=0, dz=0, dc=0):
        return (dp, slot(dx, dz, dc))

    def ydev(dy):
        return (((y + dy) % 4) * 4 + zh, f)

    def zdev(dz):
        return (y * 4 + (zh + dz) % 4, f)

    pair = fdev(dz=1)
    other = (y * 4 + (zh + 3 + 2 * zl) % 4, slot(dz=1))
    mate = fdev(dc=1)

    load_g = pltpu.make_async_copy(g_hbm, g_v, loc.at[0])
    load_g.start()
    load_s = pltpu.make_async_copy(s_hbm, s_all.at[f], loc.at[1])
    load_s.start()
    load_x = pltpu.make_async_copy(x_hbm.at[pl.ds(f * OWN, OWN)], x_all.at[f], loc.at[2])
    load_x.start()
    load_w = pltpu.make_async_copy(w_hbm, w_own, loc.at[3])
    load_w.start()

    load_m = pltpu.make_async_copy(m_hbm, m_ref, loc.at[6])
    load_m.start()
    load_v = pltpu.make_async_copy(v_hbm, v_ref, loc.at[7])
    load_v.start()

    bar = pltpu.get_barrier_semaphore()

    def greet(k, _):
        pl.semaphore_signal(bar, inc=1, device_id=(dp, (f + k) % 16), device_id_type=MESH)
        return 0

    lax.fori_loop(1, 16, greet, 0)
    for k in (1, 2, 3):
        pl.semaphore_signal(bar, inc=1, device_id=ydev(k), device_id_type=MESH)
        pl.semaphore_signal(bar, inc=1, device_id=zdev(k), device_id_type=MESH)
    pl.semaphore_signal(bar, inc=1, device_id=other, device_id_type=MESH)
    pl.semaphore_wait(bar, 22)

    def send(src, dst, ss, rs, i, to):
        cp = pltpu.make_async_remote_copy(
            src_ref=src, dst_ref=dst, send_sem=ss.at[i], recv_sem=rs.at[i],
            device_id=to, device_id_type=MESH,
        )
        cp.start()
        return cp

    def arrived(dst, ss, rs, i):
        pltpu.make_async_remote_copy(
            src_ref=dst, dst_ref=dst, send_sem=ss.at[i], recv_sem=rs.at[i],
            device_id=mate, device_id_type=MESH,
        ).wait_recv()

    sent, ysent, zsent = [], [], []
    zs = slot(dz=1)
    def rows(q):
        return pl.ds(pl.multiple_of(q * OWN, 32), OWN)

    def gather(own, at, ss, rs):
        done = []

        def go(src, dst, i, to):
            done.append(send(src, dst, ss, rs, i, to))

        def start():
            go(own, at(f), 0, pair)
            go(own, at(f), 1, fdev(dx=1))
            go(own, at(f), 2, fdev(dx=3))
            go(own, at(f), 3, mate)

        def turn_z():
            arrived(at(zs), ss, rs, 0)
            go(at(zs), at(zs), 4, fdev(dx=1))
            go(at(zs), at(zs), 5, fdev(dx=3))
            go(at(zs), at(zs), 6, mate)

        def pass_on(dz):
            base = 7 + 5 * dz
            a, b = slot(dx=3, dz=dz), slot(dx=1, dz=dz)
            arrived(at(a), ss, rs, 1 + 3 * dz)
            go(at(a, 0), at(a, 0), base, fdev(dx=1))
            arrived(at(b), ss, rs, 2 + 3 * dz)
            go(at(b, 1), at(b, 1), base + 1, fdev(dx=3))
            go(at(a), at(a), base + 2, mate)
            go(at(b), at(b), base + 3, mate)

        def pass_last(dz):
            base = 7 + 5 * dz
            q = slot(dx=2, dz=dz)
            arrived(at(q, 0), ss, rs, base)
            arrived(at(q, 1), ss, rs, base + 1)
            go(at(q), at(q), base + 4, mate)

        def finish():
            arrived(at(slot(dc=1)), ss, rs, 3)
            arrived(at(slot(dz=1, dc=1)), ss, rs, 6)
            for dz in (0, 1):
                base = 7 + 5 * dz
                arrived(at(slot(dx=3, dz=dz, dc=1)), ss, rs, base + 2)
                arrived(at(slot(dx=1, dz=dz, dc=1)), ss, rs, base + 3)
                arrived(at(slot(dx=2, dz=dz, dc=1)), ss, rs, base + 4)

        def drain():
            for cp in done:
                cp.wait_send()

        return start, turn_z, pass_on, pass_last, finish, drain

    def w_at(q, part=None):
        if part is None:
            return w_out.at[q]
        return w_out.at[q, :, part * 2048:(part + 1) * 2048]

    def span(h, part):
        if part is None:
            return slice(h * HALF, (h + 1) * HALF)
        return slice(h * HALF + part * HALF // 2, h * HALF + (part + 1) * HALF // 2)

    def c_at(h):
        return lambda q, part=None: c_all.at[rows(q), span(h, part)]

    def d_at(h):
        return lambda q, part=None: d_out.at[q, :, span(h, part)]

    cg = [gather(c_at(h)(f), c_at(h), c_ss.at[h], c_rs.at[h]) for h in range(2)]
    dg = [gather(d_own.at[:, span(h, None)], d_at(h), d_ss.at[h], d_rs.at[h]) for h in range(2)]
    w_start, w_turn, w_pass, w_last, w_finish, w_drain = gather(w_hbm, w_at, w_ss, w_rs)
    START, TURN, PASS, LAST, FINISH, DRAIN = range(6)
    own_class = (y + 2 * zl) % 4

    def rows4(off, n=None):
        base = ((own_class + off) % 4) * 64
        if n is None:
            return pl.ds(pl.multiple_of(base, 64), 64)
        return pl.ds(pl.multiple_of(base + 32 * n, 32), 32)

    mine = rows4(0)

    def s_send(src, at, i, to):
        sent.append(send(src, at, s_ss, s_rs, i, to))

    for n, to in enumerate((pair, other)):
        s_send(s_hbm.at[rows4(2, n)], s_all.at[f, rows4(2, n)], n, to)
    s_send(s_hbm.at[mine], s_all.at[f, mine], 2, fdev(dx=1))
    s_send(s_hbm.at[mine], s_all.at[f, mine], 3, fdev(dx=3))
    for n, to in enumerate((pair, other)):
        s_send(s_hbm.at[rows4(0, n)], s_all.at[f, rows4(0, n)], 4 + n, to)
    s_send(s_hbm, s_all.at[f], 6, mate)

    for n in range(2):
        arrived(s_all.at[zs, rows4(0, n)], s_ss, s_rs, n)
    s_send(s_all.at[zs, mine], s_all.at[zs, mine], 7, fdev(dx=1))
    s_send(s_all.at[zs, mine], s_all.at[zs, mine], 8, fdev(dx=3))
    s_send(s_all.at[zs, mine], s_all.at[zs, mine], 9, ydev(1))
    s_send(s_all.at[zs, mine], s_all.at[zs, mine], 10, ydev(3))

    def s_around(q, base):
        s_send(s_all.at[q, mine], s_all.at[q, mine], base, ydev(1))
        s_send(s_all.at[q, mine], s_all.at[q, mine], base + 1, ydev(3))
        s_send(s_all.at[q, rows4(0, 0)], s_all.at[q, rows4(0, 0)], base + 2, pair)
        s_send(s_all.at[q, rows4(0, 1)], s_all.at[q, rows4(0, 1)], base + 3, other)

    load_g.wait()

    def turn(t, _):
        at = pl.ds(pl.multiple_of(t * 128, 128), 128)
        gt[:, at] = g_v[at, :].T
        return 0

    by_x = []
    for dz in (0, 1):
        a, b = slot(dx=3, dz=dz), slot(dx=1, dz=dz)
        arrived(s_all.at[a, mine], s_ss, s_rs, 2 + 5 * dz)
        s_send(s_all.at[a, rows4(0, 0)], s_all.at[a, rows4(0, 0)], 12 + 2 * dz, fdev(dx=1))
        arrived(s_all.at[b, mine], s_ss, s_rs, 3 + 5 * dz)
        s_send(s_all.at[b, rows4(0, 1)], s_all.at[b, rows4(0, 1)], 13 + 2 * dz, fdev(dx=3))
        s_around(a, 20 + 10 * dz)
        s_around(b, 25 + 10 * dz)
        by_x += [(3, dz, 20 + 10 * dz), (1, dz, 25 + 10 * dz)]

    def x_send(k, _):
        p = (f + k) % 16
        send(x_hbm.at[pl.ds(p * OWN, OWN)], x_all.at[f], x_ss, x_rs, k, (dp, p))
        return 0

    lax.fori_loop(1, 16, x_send, 0)

    for dz in (0, 1):
        q = slot(dx=2, dz=dz)
        arrived(s_all.at[q, rows4(0, 0)], s_ss, s_rs, 12 + 2 * dz)
        arrived(s_all.at[q, rows4(0, 1)], s_ss, s_rs, 13 + 2 * dz)
        s_around(q, 40 + 5 * dz)
        by_x += [(2, dz, 40 + 5 * dz)]
    lax.fori_loop(0, 12, turn, 0)

    arrived(s_all.at[zs, rows4(2, 0)], s_ss, s_rs, 4)
    arrived(s_all.at[zs, rows4(2, 1)], s_ss, s_rs, 5)
    arrived(s_all.at[zs, rows4(3)], s_ss, s_rs, 9)
    arrived(s_all.at[zs, rows4(1)], s_ss, s_rs, 10)
    s_send(s_all.at[zs], s_all.at[zs], 11, mate)
    base_of = {(dx, dz): base for dx, dz, base in by_x}
    for dx, dz, base in by_x:
        q = slot(dx=dx, dz=dz)
        arrived(s_all.at[q, rows4(3)], s_ss, s_rs, base)
        arrived(s_all.at[q, rows4(1)], s_ss, s_rs, base + 1)
        came = base_of[dx, 1 - dz]
        arrived(s_all.at[q, rows4(2, 0)], s_ss, s_rs, came + 2)
        arrived(s_all.at[q, rows4(2, 1)], s_ss, s_rs, came + 3)
        s_send(s_all.at[q], s_all.at[q], base + 4, mate)
    arrived(s_all.at[slot(dc=1)], s_ss, s_rs, 6)
    arrived(s_all.at[slot(dz=1, dc=1)], s_ss, s_rs, 11)
    for dx, dz, base in by_x:
        arrived(s_all.at[slot(dx=dx, dz=dz, dc=1)], s_ss, s_rs, base + 4)

    def x_wait(k, _):
        arrived(x_all.at[(f + 16 - k) % 16], x_ss, x_rs, k)
        return 0

    lax.fori_loop(1, 16, x_wait, 0)
    def x_sent(k, _):
        pltpu.make_async_remote_copy(
            src_ref=x_hbm.at[pl.ds(0, OWN)], dst_ref=x_all.at[0], send_sem=x_ss.at[k], recv_sem=x_rs.at[k],
            device_id=mate, device_id_type=MESH,
        ).wait_send()
        return 0

    lax.fori_loop(1, 16, x_sent, 0)
    load_s.wait()
    load_x.wait()
    load_m.wait()
    load_v.wait()
    keep_s = pltpu.make_async_copy(s_all, s_out, loc.at[4])
    keep_s.start()

    acc[...] = jnp.zeros_like(acc)

    def add(i, _):
        acc[...] += jnp.dot(x_all[i], s_all[i], preferred_element_type=F32)
        return 0

    lax.fori_loop(0, 16, add, 0)

    c_all[rows(f), :] = acc[...].astype(BF)

    def block(k, p):
        t = (y + k) % 4
        a = gt[pl.ds(pl.multiple_of(t * YROWS, 32), YROWS), :]
        return jnp.dot(a, c_all[:, p * PART:(p + 1) * PART], preferred_element_type=F32)

    def y_start(p):
        for k in (1, 3, 2):
            ysend[p, k - 1] = block(k, p).astype(BF)
            ysent.append(send(ysend.at[p, k - 1], yrecv.at[p, k - 1], y_ss, y_rs, 3 * p + k - 1, ydev(k)))
        yown[p] = block(0, p)

    def z_start(p):
        for k in (1, 3, 2):
            arrived(yrecv.at[p, k - 1], y_ss, y_rs, 3 * p + k - 1)
        yown[p] = yown[p] + yrecv[p, 0].astype(F32) + yrecv[p, 1].astype(F32) + yrecv[p, 2].astype(F32)
        for k in (1, 3, 2):
            t = (zh + k) % 4
            src = yown.at[p, pl.ds(pl.multiple_of(t * UNITS, 8), UNITS)]
            zsent.append(send(src, zrecv.at[p, k - 1], z_ss, z_rs, 3 * p + k - 1, zdev(k)))

    def step(p):
        cols = slice(p * PART, (p + 1) * PART)
        for k in (1, 3, 2):
            arrived(zrecv.at[p, k - 1], z_ss, z_rs, 3 * p + k - 1)
        got = yown[p, pl.ds(pl.multiple_of(zh * UNITS, 8), UNITS), :]
        got = got + zrecv[p, 0] + zrecv[p, 1] + zrecv[p, 2]
        p_out[:, cols] = got
        one = beta_one * m_ref[:, cols] + (1.0 - beta_one) * got
        two = beta_two * v_ref[:, cols] + (1.0 - beta_two) * got * got
        d_own[:, cols] = (one / bias_one / (jnp.sqrt(two / bias_two) + epsilon)).astype(BF)

    c0, c1 = cg
    d0, d1 = dg
    c0[START]()
    c0[TURN]()
    c1[START]()
    c1[TURN]()
    c0[PASS](0)
    c0[PASS](1)
    c0[LAST](0)
    c0[LAST](1)
    c1[PASS](0)
    c1[PASS](1)
    w_start()
    load_w.wait()
    keep_w = pltpu.make_async_copy(w_own, w_out.at[f], loc.at[8])
    keep_w.start()
    c0[FINISH]()
    y_start(0)
    y_start(1)
    c1[LAST](0)
    c1[LAST](1)
    c1[FINISH]()
    y_start(2)
    y_start(3)
    w_turn()
    z_start(0)
    z_start(1)
    w_pass(0)
    z_start(2)
    step(0)
    step(1)
    d0[START]()
    z_start(3)
    d0[TURN]()
    w_pass(1)
    step(2)
    step(3)
    d1[START]()
    d0[PASS](0)
    d0[PASS](1)
    d1[TURN]()
    keep_d = pltpu.make_async_copy(d_own, d_out.at[f], loc.at[5])
    keep_d.start()
    w_last(0)
    d0[LAST](0)
    d0[LAST](1)
    d1[PASS](0)
    d1[PASS](1)
    w_last(1)
    d1[LAST](0)
    d1[LAST](1)
    w_finish()
    d0[FINISH]()
    d1[FINISH]()
    keep_d.wait()
    keep_w.wait()
    w_drain()
    for g in cg + dg:
        g[DRAIN]()
    keep_s.wait()
    for cp in sent + ysent + zsent:
        cp.wait_send()


def exchange(layer_input, grad_out, subspace, up_weight, first, second):
    hbm = pl.BlockSpec(memory_space=pl.ANY)
    vmem = pl.BlockSpec(memory_space=pltpu.VMEM)
    dma = pltpu.SemaphoreType.DMA
    return pl.pallas_call(
        body,
        out_shape=(
            jax.ShapeDtypeStruct((16, DIN, R), BF),
            jax.ShapeDtypeStruct((16, UNITS, 4096), BF),
            jax.ShapeDtypeStruct((16, UNITS, R), BF),
            jax.ShapeDtypeStruct((UNITS, R), F32),
        ),
        in_specs=[hbm] * 6,
        out_specs=(hbm, hbm, hbm, vmem),
        scratch_shapes=[
            pltpu.VMEM((16, DIN, R), BF),
            pltpu.VMEM((16, OWN, DIN), BF),
            pltpu.VMEM((TOK, HID), BF),
            pltpu.VMEM((HID, TOK), BF),
            pltpu.VMEM((TOK, R), BF),
            pltpu.VMEM((OWN, R), F32),
            pltpu.VMEM((PARTS, 3, YROWS, PART), BF),
            pltpu.VMEM((PARTS, 3, YROWS, PART), BF),
            pltpu.VMEM((PARTS, YROWS, PART), F32),
            pltpu.VMEM((PARTS, 3, UNITS, PART), F32),
            pltpu.VMEM((UNITS, R), BF),
            pltpu.VMEM((UNITS, R), F32),
            pltpu.VMEM((UNITS, R), F32),
            pltpu.VMEM((UNITS, 4096), BF),
            dma((9,)),
            dma((50,)), dma((50,)),
            dma((16,)), dma((16,)),
            dma((2, 17)), dma((2, 17)),
            dma((17,)), dma((17,)),
            dma((2, 17)), dma((2, 17)),
            dma((3 * PARTS,)), dma((3 * PARTS,)),
            dma((3 * PARTS,)), dma((3 * PARTS,)),
        ],
        compiler_params=pltpu.CompilerParams(
            collective_id=0, has_side_effects=True, vmem_limit_bytes=60 * 2**20
        ),
        cost_estimate=pl.CostEstimate(flops=4 * 10**9, bytes_accessed=4 * 10**7, transcendentals=0),
        name="exchange",
    )(layer_input, grad_out, subspace, up_weight, first, second)


def finish(d_ref, s_ref, w_ref, p_ref, m_ref, v_ref, o_ref, one_ref, two_ref):
    @pl.when(pl.program_id(0) == 0)
    def _():
        got = p_ref[...]
        one_ref[...] = beta_one * m_ref[...] + (1.0 - beta_one) * got
        two_ref[...] = beta_two * v_ref[...] + (1.0 - beta_two) * got * got

    change = lax.dot_general(
        d_ref[...], s_ref[...], (((1,), (1,)), ((), ())), preferred_element_type=F32
    )
    o_ref[...] = (w_ref[...].astype(F32) - step_size * change).astype(BF)


TILE = 1024


def update(direction, basis, weights, projected, first, second):
    whole = pl.BlockSpec((UNITS, R), lambda i: (0, 0))
    return pl.pallas_call(
        finish,
        grid=(4096 // TILE,),
        out_shape=(
            jax.ShapeDtypeStruct((HID, 4096), BF),
            jax.ShapeDtypeStruct((UNITS, R), F32),
            jax.ShapeDtypeStruct((UNITS, R), F32),
        ),
        in_specs=[
            pl.BlockSpec((HID, R), lambda i: (0, 0)),
            pl.BlockSpec((TILE, R), lambda i: (i, 0)),
            pl.BlockSpec((HID, TILE), lambda i: (0, i)),
            whole, whole, whole,
        ],
        out_specs=(pl.BlockSpec((HID, TILE), lambda i: (0, i)), whole, whole),
        compiler_params=pltpu.CompilerParams(vmem_limit_bytes=60 * 2**20),
        cost_estimate=pl.CostEstimate(flops=8 * 10**9, bytes_accessed=26 * 10**6, transcendentals=0),
        name="update",
    )(direction, basis, weights, projected, first, second)


def local(layer_input, grad_out, subspace, up_weight, first_moment, second_moment):
    basis, weights, direction, projected = exchange(
        layer_input, grad_out, subspace, up_weight[0], first_moment[0], second_moment[0]
    )
    updated, moment_one, moment_two = update(
        direction.reshape(HID, R), basis.reshape(4096, R), weights.reshape(HID, 4096),
        projected, first_moment[0], second_moment[0],
    )
    return (updated.reshape(16, UNITS, 4096), moment_one[None], moment_two[None])


def solution(mesh):
    placed = (
        P("dp", "fsdp"),
        P("dp", "fsdp"),
        P("fsdp", None),
        P("fsdp", "dp", None),
        P("fsdp", "dp", None),
        P("fsdp", "dp", None),
    )
    return jax.shard_map(
        local,
        mesh=mesh,
        in_specs=placed,
        out_specs=(P(None, "dp", None), P("fsdp", "dp", None), P("fsdp", "dp", None)),
        check_vma=False,
    )
```

```python
import jax
import jax.numpy as jnp
from jax import lax
from jax.experimental import pallas as pl
from jax.experimental.pallas import tpu as pltpu
from jax.sharding import PartitionSpec as P

beta_one = 0.9
beta_two = 0.999
bias_one = 1.0 - 0.9**10
bias_two = 1.0 - 0.999**10
epsilon = 1e-08
step_size = 0.05

MESH = pl.DeviceIdType.MESH
BF = jnp.bfloat16
F32 = jnp.float32

TOK = 1536
OWN = 96
DIN = 256
R = 1024
HID = 896
UNITS = 56
YROWS = 224
HALF = 512
PARTS = 4
PART = R // PARTS


def body(
    x_hbm, g_hbm, s_hbm, w_hbm, m_hbm, v_hbm,
    s_out, w_out, d_out, p_out,
    s_all, x_all, g_v, gt, c_all, acc, ysend, yrecv, yown, zrecv, d_own, m_ref, v_ref, w_own,
    loc, s_ss, s_rs, x_ss, x_rs, c_ss, c_rs, w_ss, w_rs, d_ss, d_rs, y_ss, y_rs, z_ss, z_rs,
):
    dp = lax.axis_index("dp")
    f = lax.axis_index("fsdp")
    y, zh = dp // 4, dp % 4
    x, zl, c = f // 4, (f // 2) % 2, f % 2

    def slot(dx=0, dz=0, dc=0):
        xx = (x + dx) % 4
        zz = (zl + dz) % 2
        cc = (c + dc) % 2
        return xx * 4 + zz * 2 + cc

    def fdev(dx=0, dz=0, dc=0):
        return (dp, slot(dx, dz, dc))

    def ydev(dy):
        return (((y + dy) % 4) * 4 + zh, f)

    def zdev(dz):
        return (y * 4 + (zh + dz) % 4, f)

    pair = fdev(dz=1)
    other = (y * 4 + (zh + 3 + 2 * zl) % 4, slot(dz=1))
    mate = fdev(dc=1)

    load_g = pltpu.make_async_copy(g_hbm, g_v, loc.at[0])
    load_g.start()
    load_s = pltpu.make_async_copy(s_hbm, s_all.at[f], loc.at[1])
    load_s.start()
    load_x = pltpu.make_async_copy(x_hbm.at[pl.ds(f * OWN, OWN)], x_all.at[f], loc.at[2])
    load_x.start()
    load_w = pltpu.make_async_copy(w_hbm, w_own, loc.at[3])
    load_w.start()

    load_m = pltpu.make_async_copy(m_hbm, m_ref, loc.at[6])
    load_m.start()
    load_v = pltpu.make_async_copy(v_hbm, v_ref, loc.at[7])
    load_v.start()

    bar = pltpu.get_barrier_semaphore()

    def greet(k, _):
        pl.semaphore_signal(bar, inc=1, device_id=(dp, (f + k) % 16), device_id_type=MESH)
        return 0

    lax.fori_loop(1, 16, greet, 0)
    for k in (1, 2, 3):
        pl.semaphore_signal(bar, inc=1, device_id=ydev(k), device_id_type=MESH)
        pl.semaphore_signal(bar, inc=1, device_id=zdev(k), device_id_type=MESH)
    pl.semaphore_signal(bar, inc=1, device_id=other, device_id_type=MESH)
    pl.semaphore_wait(bar, 22)

    def send(src, dst, ss, rs, i, to):
        cp = pltpu.make_async_remote_copy(
            src_ref=src, dst_ref=dst, send_sem=ss.at[i], recv_sem=rs.at[i],
            device_id=to, device_id_type=MESH,
        )
        cp.start()
        return cp

    def arrived(dst, ss, rs, i):
        pltpu.make_async_remote_copy(
            src_ref=dst, dst_ref=dst, send_sem=ss.at[i], recv_sem=rs.at[i],
            device_id=mate, device_id_type=MESH,
        ).wait_recv()

    sent, ysent, zsent = [], [], []
    zs = slot(dz=1)
    def rows(q):
        return pl.ds(pl.multiple_of(q * OWN, 32), OWN)

    def gather(own, at, ss, rs):
        done = []

        def go(src, dst, i, to):
            done.append(send(src, dst, ss, rs, i, to))

        def start():
            go(own, at(f), 0, pair)
            go(own, at(f), 1, fdev(dx=1))
            go(own, at(f), 2, fdev(dx=3))
            go(own, at(f), 3, mate)

        def turn_z():
            arrived(at(zs), ss, rs, 0)
            go(at(zs), at(zs), 4, fdev(dx=1))
            go(at(zs), at(zs), 5, fdev(dx=3))
            go(at(zs), at(zs), 6, mate)

        def pass_on(dz):
            base = 7 + 5 * dz
            a, b = slot(dx=3, dz=dz), slot(dx=1, dz=dz)
            arrived(at(a), ss, rs, 1 + 3 * dz)
            go(at(a, 0), at(a, 0), base, fdev(dx=1))
            arrived(at(b), ss, rs, 2 + 3 * dz)
            go(at(b, 1), at(b, 1), base + 1, fdev(dx=3))
            go(at(a), at(a), base + 2, mate)
            go(at(b), at(b), base + 3, mate)

        def pass_last(dz):
            base = 7 + 5 * dz
            q = slot(dx=2, dz=dz)
            arrived(at(q, 0), ss, rs, base)
            arrived(at(q, 1), ss, rs, base + 1)
            go(at(q), at(q), base + 4, mate)

        def finish():
            arrived(at(slot(dc=1)), ss, rs, 3)
            arrived(at(slot(dz=1, dc=1)), ss, rs, 6)
            for dz in (0, 1):
                base = 7 + 5 * dz
                arrived(at(slot(dx=3, dz=dz, dc=1)), ss, rs, base + 2)
                arrived(at(slot(dx=1, dz=dz, dc=1)), ss, rs, base + 3)
                arrived(at(slot(dx=2, dz=dz, dc=1)), ss, rs, base + 4)

        def drain():
            for cp in done:
                cp.wait_send()

        return start, turn_z, pass_on, pass_last, finish, drain

    def w_at(q, part=None):
        if part is None:
            return w_out.at[q]
        return w_out.at[q, :, part * 2048:(part + 1) * 2048]

    def span(h, part):
        if part is None:
            return slice(h * HALF, (h + 1) * HALF)
        return slice(h * HALF + part * HALF // 2, h * HALF + (part + 1) * HALF // 2)

    def c_at(h):
        return lambda q, part=None: c_all.at[rows(q), span(h, part)]

    def d_at(h):
        return lambda q, part=None: d_out.at[q, :, span(h, part)]

    cg = [gather(c_at(h)(f), c_at(h), c_ss.at[h], c_rs.at[h]) for h in range(2)]
    dg = [gather(d_own.at[:, span(h, None)], d_at(h), d_ss.at[h], d_rs.at[h]) for h in range(2)]
    w_start, w_turn, w_pass, w_last, w_finish, w_drain = gather(w_hbm, w_at, w_ss, w_rs)
    START, TURN, PASS, LAST, FINISH, DRAIN = range(6)
    own_class = (y + 2 * zl) % 4

    def rows4(off, n=None):
        base = ((own_class + off) % 4) * 64
        if n is None:
            return pl.ds(pl.multiple_of(base, 64), 64)
        return pl.ds(pl.multiple_of(base + 32 * n, 32), 32)

    mine = rows4(0)

    def s_send(src, at, i, to):
        sent.append(send(src, at, s_ss, s_rs, i, to))

    for n, to in enumerate((pair, other)):
        s_send(s_hbm.at[rows4(2, n)], s_all.at[f, rows4(2, n)], n, to)
    s_send(s_hbm.at[mine], s_all.at[f, mine], 2, fdev(dx=1))
    s_send(s_hbm.at[mine], s_all.at[f, mine], 3, fdev(dx=3))
    for n, to in enumerate((pair, other)):
        s_send(s_hbm.at[rows4(0, n)], s_all.at[f, rows4(0, n)], 4 + n, to)
    s_send(s_hbm, s_all.at[f], 6, mate)

    for n in range(2):
        arrived(s_all.at[zs, rows4(0, n)], s_ss, s_rs, n)
    s_send(s_all.at[zs, mine], s_all.at[zs, mine], 7, fdev(dx=1))
    s_send(s_all.at[zs, mine], s_all.at[zs, mine], 8, fdev(dx=3))
    s_send(s_all.at[zs, mine], s_all.at[zs, mine], 9, ydev(1))
    s_send(s_all.at[zs, mine], s_all.at[zs, mine], 10, ydev(3))

    def s_around(q, base):
        s_send(s_all.at[q, mine], s_all.at[q, mine], base, ydev(1))
        s_send(s_all.at[q, mine], s_all.at[q, mine], base + 1, ydev(3))
        s_send(s_all.at[q, rows4(0, 0)], s_all.at[q, rows4(0, 0)], base + 2, pair)
        s_send(s_all.at[q, rows4(0, 1)], s_all.at[q, rows4(0, 1)], base + 3, other)

    load_g.wait()

    def turn(t, _):
        at = pl.ds(pl.multiple_of(t * 128, 128), 128)
        gt[:, at] = g_v[at, :].T
        return 0

    by_x = []
    for dz in (0, 1):
        a, b = slot(dx=3, dz=dz), slot(dx=1, dz=dz)
        arrived(s_all.at[a, mine], s_ss, s_rs, 2 + 5 * dz)
        s_send(s_all.at[a, rows4(0, 0)], s_all.at[a, rows4(0, 0)], 12 + 2 * dz, fdev(dx=1))
        arrived(s_all.at[b, mine], s_ss, s_rs, 3 + 5 * dz)
        s_send(s_all.at[b, rows4(0, 1)], s_all.at[b, rows4(0, 1)], 13 + 2 * dz, fdev(dx=3))
        s_around(a, 20 + 10 * dz)
        s_around(b, 25 + 10 * dz)
        by_x += [(3, dz, 20 + 10 * dz), (1, dz, 25 + 10 * dz)]

    def x_send(k, _):
        p = (f + k) % 16
        send(x_hbm.at[pl.ds(p * OWN, OWN)], x_all.at[f], x_ss, x_rs, k, (dp, p))
        return 0

    lax.fori_loop(1, 16, x_send, 0)

    for dz in (0, 1):
        q = slot(dx=2, dz=dz)
        arrived(s_all.at[q, rows4(0, 0)], s_ss, s_rs, 12 + 2 * dz)
        arrived(s_all.at[q, rows4(0, 1)], s_ss, s_rs, 13 + 2 * dz)
        s_around(q, 40 + 5 * dz)
        by_x += [(2, dz, 40 + 5 * dz)]
    lax.fori_loop(0, 12, turn, 0)

    arrived(s_all.at[zs, rows4(2, 0)], s_ss, s_rs, 4)
    arrived(s_all.at[zs, rows4(2, 1)], s_ss, s_rs, 5)
    arrived(s_all.at[zs, rows4(3)], s_ss, s_rs, 9)
    arrived(s_all.at[zs, rows4(1)], s_ss, s_rs, 10)
    s_send(s_all.at[zs], s_all.at[zs], 11, mate)
    base_of = {(dx, dz): base for dx, dz, base in by_x}
    for dx, dz, base in by_x:
        q = slot(dx=dx, dz=dz)
        arrived(s_all.at[q, rows4(3)], s_ss, s_rs, base)
        arrived(s_all.at[q, rows4(1)], s_ss, s_rs, base + 1)
        came = base_of[dx, 1 - dz]
        arrived(s_all.at[q, rows4(2, 0)], s_ss, s_rs, came + 2)
        arrived(s_all.at[q, rows4(2, 1)], s_ss, s_rs, came + 3)
        s_send(s_all.at[q], s_all.at[q], base + 4, mate)
    arrived(s_all.at[slot(dc=1)], s_ss, s_rs, 6)
    arrived(s_all.at[slot(dz=1, dc=1)], s_ss, s_rs, 11)
    for dx, dz, base in by_x:
        arrived(s_all.at[slot(dx=dx, dz=dz, dc=1)], s_ss, s_rs, base + 4)

    def x_wait(k, _):
        arrived(x_all.at[(f + 16 - k) % 16], x_ss, x_rs, k)
        return 0

    lax.fori_loop(1, 16, x_wait, 0)
    def x_sent(k, _):
        pltpu.make_async_remote_copy(
            src_ref=x_hbm.at[pl.ds(0, OWN)], dst_ref=x_all.at[0], send_sem=x_ss.at[k], recv_sem=x_rs.at[k],
            device_id=mate, device_id_type=MESH,
        ).wait_send()
        return 0

    lax.fori_loop(1, 16, x_sent, 0)
    load_s.wait()
    load_x.wait()
    load_m.wait()
    load_v.wait()
    keep_s = pltpu.make_async_copy(s_all, s_out, loc.at[4])
    keep_s.start()

    acc[...] = jnp.zeros_like(acc)

    def add(i, _):
        acc[...] += jnp.dot(x_all[i], s_all[i], preferred_element_type=F32)
        return 0

    lax.fori_loop(0, 16, add, 0)

    c_all[rows(f), :] = acc[...].astype(BF)

    def block(k, p):
        t = (y + k) % 4
        a = gt[pl.ds(pl.multiple_of(t * YROWS, 32), YROWS), :]
        return jnp.dot(a, c_all[:, p * PART:(p + 1) * PART], preferred_element_type=F32)

    def y_start(p):
        for k in (1, 3, 2):
            ysend[p, k - 1] = block(k, p).astype(BF)
            ysent.append(send(ysend.at[p, k - 1], yrecv.at[p, k - 1], y_ss, y_rs, 3 * p + k - 1, ydev(k)))

    def y_own(p):
        yown[p] = block(0, p)

    def z_start(p):
        for k in (1, 3, 2):
            arrived(yrecv.at[p, k - 1], y_ss, y_rs, 3 * p + k - 1)
        yown[p] = yown[p] + yrecv[p, 0].astype(F32) + yrecv[p, 1].astype(F32) + yrecv[p, 2].astype(F32)
        for k in (1, 3, 2):
            t = (zh + k) % 4
            src = yown.at[p, pl.ds(pl.multiple_of(t * UNITS, 8), UNITS)]
            zsent.append(send(src, zrecv.at[p, k - 1], z_ss, z_rs, 3 * p + k - 1, zdev(k)))

    def step(p):
        cols = slice(p * PART, (p + 1) * PART)
        for k in (1, 3, 2):
            arrived(zrecv.at[p, k - 1], z_ss, z_rs, 3 * p + k - 1)
        got = yown[p, pl.ds(pl.multiple_of(zh * UNITS, 8), UNITS), :]
        got = got + zrecv[p, 0] + zrecv[p, 1] + zrecv[p, 2]
        p_out[:, cols] = got
        one = beta_one * m_ref[:, cols] + (1.0 - beta_one) * got
        two = beta_two * v_ref[:, cols] + (1.0 - beta_two) * got * got
        d_own[:, cols] = (one / bias_one / (jnp.sqrt(two / bias_two) + epsilon)).astype(BF)

    c0, c1 = cg
    d0, d1 = dg
    c0[START]()
    c0[TURN]()
    c1[START]()
    c1[TURN]()
    c0[PASS](0)
    c0[PASS](1)
    c0[LAST](0)
    c0[LAST](1)
    c1[PASS](0)
    c1[PASS](1)
    w_start()
    load_w.wait()
    keep_w = pltpu.make_async_copy(w_own, w_out.at[f], loc.at[8])
    keep_w.start()
    c0[FINISH]()
    y_start(0)
    y_start(1)
    y_own(0)
    y_own(1)
    c1[LAST](0)
    c1[LAST](1)
    c1[FINISH]()
    y_start(2)
    y_start(3)
    w_turn()
    y_own(2)
    y_own(3)
    z_start(0)
    z_start(1)
    w_pass(0)
    z_start(2)
    step(0)
    step(1)
    d0[START]()
    z_start(3)
    d0[TURN]()
    w_pass(1)
    step(2)
    step(3)
    d1[START]()
    d0[PASS](0)
    d0[PASS](1)
    d1[TURN]()
    keep_d = pltpu.make_async_copy(d_own, d_out.at[f], loc.at[5])
    keep_d.start()
    w_last(0)
    d0[LAST](0)
    d0[LAST](1)
    d1[PASS](0)
    d1[PASS](1)
    w_last(1)
    d1[LAST](0)
    d1[LAST](1)
    w_finish()
    d0[FINISH]()
    d1[FINISH]()
    keep_d.wait()
    keep_w.wait()
    w_drain()
    for g in cg + dg:
        g[DRAIN]()
    keep_s.wait()
    for cp in sent + ysent + zsent:
        cp.wait_send()


def exchange(layer_input, grad_out, subspace, up_weight, first, second):
    hbm = pl.BlockSpec(memory_space=pl.ANY)
    vmem = pl.BlockSpec(memory_space=pltpu.VMEM)
    dma = pltpu.SemaphoreType.DMA
    return pl.pallas_call(
        body,
        out_shape=(
            jax.ShapeDtypeStruct((16, DIN, R), BF),
            jax.ShapeDtypeStruct((16, UNITS, 4096), BF),
            jax.ShapeDtypeStruct((16, UNITS, R), BF),
            jax.ShapeDtypeStruct((UNITS, R), F32),
        ),
        in_specs=[hbm] * 6,
        out_specs=(hbm, hbm, hbm, vmem),
        scratch_shapes=[
            pltpu.VMEM((16, DIN, R), BF),
            pltpu.VMEM((16, OWN, DIN), BF),
            pltpu.VMEM((TOK, HID), BF),
            pltpu.VMEM((HID, TOK), BF),
            pltpu.VMEM((TOK, R), BF),
            pltpu.VMEM((OWN, R), F32),
            pltpu.VMEM((PARTS, 3, YROWS, PART), BF),
            pltpu.VMEM((PARTS, 3, YROWS, PART), BF),
            pltpu.VMEM((PARTS, YROWS, PART), F32),
            pltpu.VMEM((PARTS, 3, UNITS, PART), F32),
            pltpu.VMEM((UNITS, R), BF),
            pltpu.VMEM((UNITS, R), F32),
            pltpu.VMEM((UNITS, R), F32),
            pltpu.VMEM((UNITS, 4096), BF),
            dma((9,)),
            dma((50,)), dma((50,)),
            dma((16,)), dma((16,)),
            dma((2, 17)), dma((2, 17)),
            dma((17,)), dma((17,)),
            dma((2, 17)), dma((2, 17)),
            dma((3 * PARTS,)), dma((3 * PARTS,)),
            dma((3 * PARTS,)), dma((3 * PARTS,)),
        ],
        compiler_params=pltpu.CompilerParams(
            collective_id=0, has_side_effects=True, vmem_limit_bytes=60 * 2**20
        ),
        cost_estimate=pl.CostEstimate(flops=4 * 10**9, bytes_accessed=4 * 10**7, transcendentals=0),
        name="exchange",
    )(layer_input, grad_out, subspace, up_weight, first, second)


def finish(d_ref, s_ref, w_ref, p_ref, m_ref, v_ref, o_ref, one_ref, two_ref):
    @pl.when(pl.program_id(0) == 0)
    def _():
        got = p_ref[...]
        one_ref[...] = beta_one * m_ref[...] + (1.0 - beta_one) * got
        two_ref[...] = beta_two * v_ref[...] + (1.0 - beta_two) * got * got

    change = lax.dot_general(
        d_ref[...], s_ref[...], (((1,), (1,)), ((), ())), preferred_element_type=F32
    )
    o_ref[...] = (w_ref[...].astype(F32) - step_size * change).astype(BF)


TILE = 1024


def update(direction, basis, weights, projected, first, second):
    whole = pl.BlockSpec((UNITS, R), lambda i: (0, 0))
    return pl.pallas_call(
        finish,
        grid=(4096 // TILE,),
        out_shape=(
            jax.ShapeDtypeStruct((HID, 4096), BF),
            jax.ShapeDtypeStruct((UNITS, R), F32),
            jax.ShapeDtypeStruct((UNITS, R), F32),
        ),
        in_specs=[
            pl.BlockSpec((HID, R), lambda i: (0, 0)),
            pl.BlockSpec((TILE, R), lambda i: (i, 0)),
            pl.BlockSpec((HID, TILE), lambda i: (0, i)),
            whole, whole, whole,
        ],
        out_specs=(pl.BlockSpec((HID, TILE), lambda i: (0, i)), whole, whole),
        compiler_params=pltpu.CompilerParams(vmem_limit_bytes=60 * 2**20),
        cost_estimate=pl.CostEstimate(flops=8 * 10**9, bytes_accessed=26 * 10**6, transcendentals=0),
        name="update",
    )(direction, basis, weights, projected, first, second)


def local(layer_input, grad_out, subspace, up_weight, first_moment, second_moment):
    basis, weights, direction, projected = exchange(
        layer_input, grad_out, subspace, up_weight[0], first_moment[0], second_moment[0]
    )
    updated, moment_one, moment_two = update(
        direction.reshape(HID, R), basis.reshape(4096, R), weights.reshape(HID, 4096),
        projected, first_moment[0], second_moment[0],
    )
    return (updated.reshape(16, UNITS, 4096), moment_one[None], moment_two[None])


def solution(mesh):
    placed = (
        P("dp", "fsdp"),
        P("dp", "fsdp"),
        P("fsdp", None),
        P("fsdp", "dp", None),
        P("fsdp", "dp", None),
        P("fsdp", "dp", None),
    )
    return jax.shard_map(
        local,
        mesh=mesh,
        in_specs=placed,
        out_specs=(P(None, "dp", None), P("fsdp", "dp", None), P("fsdp", "dp", None)),
        check_vma=False,
    )
```
